32 devices in a mesh: seq: 8 (over z, core), tp: 4 (over y, x).
Axes of the slice: x: 2, y: 2, z: 4, core: 2. Of those that a mesh axis runs over, the one named last changes fastest.
Arguments:
- trainer_rows: float32 [2, 1024, 12544], P(None, ('seq', 'tp')), as said below
- shard_order: int32 [32], replicated, may hold values from 0 to 31, each once
- residual_in: float32 [8192, 1024], P(('seq', 'tp')), may hold values from -6 to 6
- norm_gains: float32 [2, 2, 1024], replicated, may hold values from 0.25 to 1.75
- prompt_lengths: int32 [8, 4], P('seq'), may hold values from 1 to 512, 1024 in all within a row
- variate_ids: int32 [8192], P('seq'), may hold values from 0 to 7
- variate_bias: float32 [2, 16, 2], replicated, may hold values from -2 to 260
Outputs:
- hidden_states: float32 [8192, 1024], P(('seq', 'tp'))
The draws below stay inside these ranges and needn't reach their ends.
Inputs may be any that keep to these rules, and one draw needn't show every extreme that they name: shard_order is a permutation of the trainer shards' row blocks. `prompt_lengths`: each row sums to 1024, and one entry of each row is 512. `trainer_rows`: entries of columns up to 9728 are at most 6 / sqrt(1024) in size, later ones at most 6 / sqrt(2816).
All inputs are finite; a program needn't handle non-finite values.
Results may differ from the reference program's by a relative error of at most 0.017.
Values may be sent and summed in bfloat16 or wider, within the bound.
A program may use at most 128 MiB of HBM per device.

```python
import math
import jax
import jax.numpy as jnp
import numpy as np
from jax import lax

D = 1024
H = 16
HD = 64
FF = 2816
LAYERS = 2
NVAR = 8
LEN = 512
TOK_DEV = 1024
PROMPTS_DEV = 4
TOKENS = 8192
N_SEQ = 8
N_TP = 4
DEVICES = 32


def draw_trainer_rows(key, part):
    values = jnp.clip(jax.random.normal(key, (LAYERS, D, 4 * D + 3 * FF), jnp.float32), -6.0, 6.0)
    column = jnp.arange(4 * D + 3 * FF)
    scales = jnp.where(column >= 4 * D + 2 * FF, FF ** (-0.5), D ** (-0.5)).astype(jnp.float32)
    return values * scales[None, None, :]


def draw_variate_bias(key, part):
    key_base = jax.random.fold_in(key, 11)
    offsets = jax.random.uniform(key_base, (LAYERS, H, 2), jnp.float32, -2.0, 2.0)
    return offsets


def set_ends(values, stream_key, low, largest):
    spot = [jax.random.randint(jax.random.fold_in(stream_key, axis), (), 0, length) for axis, length in enumerate(values.shape)]
    main_axis = values.shape.index(max(values.shape))
    neighbour = spot[:main_axis] + [(spot[main_axis] + 1) % values.shape[main_axis]] + spot[main_axis + 1:]
    return values.at[tuple(spot)].set(low).at[tuple(neighbour)].set(largest)


def steps_of(own_key, extent, split, least, high):
    def one(position, shards_of):
        heights = jax.random.uniform(jax.random.fold_in(jax.random.fold_in(own_key, 6), position), (shards_of,), jnp.float32, least / len(split), high / len(split))
        return jnp.repeat(jnp.exp(heights), extent[position] // shards_of).reshape((-1,) + (1,) * (len(extent) - position - 1))

    level = one(*split[0])
    for cut in split[1:]:
        level = level * one(*cut)
    return level


def split_up(amount, total, reach, lean):
    loads = [(1 << 20) // math.isqrt(grade ** lean) + 1 for grade in range(2, amount + 1)]
    rest, counts = total - reach - (amount - 1), [1] * (amount - 1)
    while rest > 0:
        candidates = [i for i in range(amount - 1) if counts[i] < reach]
        mass, remaining = sum([loads[i] for i in candidates]), rest
        for i in candidates:
            extra = min(reach - counts[i], max(1, remaining * loads[i] // mass), rest)
            counts[i] = counts[i] + extra
            rest = rest - extra
    return np.array([reach] + counts)


def uneven(stream_key, number_of, total, bound, lean):
    if number_of == 2:
        one = jax.random.randint(stream_key, (), max(1, total - bound), min(bound, total - 1) + 1)
        return jnp.stack([one, total - one])
    sizes = jnp.asarray(split_up(number_of, total, bound, lean), jnp.int32)
    pairs = (number_of - 1) // 2
    source_of, sink = sizes[1:1 + 2 * pairs:2], sizes[2:2 + 2 * pairs:2]
    slack = jnp.minimum(source_of - 1, bound - sink)
    passed = jax.random.randint(jax.random.fold_in(stream_key, 1), (pairs,), 0, 1 << 20) % (slack + 1)
    sizes = sizes.at[1:1 + 2 * pairs:2].set(source_of - passed).at[2:2 + 2 * pairs:2].set(sink + passed)
    return sizes[jax.random.permutation(jax.random.fold_in(stream_key, 2), number_of)]


def scatter_about(rng, shape, scale, bound, split=(), kind=jnp.bfloat16):
    array = scale * jax.random.normal(rng, shape, jnp.float32)
    if split:
        array = array * steps_of(rng, shape, split, -0.22, 0.18)
    return jnp.clip(array, -bound, bound).astype(kind)


def setup_inputs(seed: int = 0) -> dict:
    arg_keys = jax.random.split(jax.random.key(seed), 8)
    trainer_rows = draw_trainer_rows(jax.random.fold_in(arg_keys[7], 71), 0)
    shard_order = jax.random.permutation(arg_keys[1], DEVICES).astype(jnp.int32)
    residual_in = scatter_about(arg_keys[2], (TOKENS, D), 1.0, 6.0, ((0, 32),), jnp.float32)
    norm_gains = jnp.clip(1.0 + 0.15 * jax.random.normal(arg_keys[3], (LAYERS, 2, D), jnp.float32), 0.25, 1.75)
    prompt_lengths = jax.vmap(lambda own: uneven(own, PROMPTS_DEV, TOK_DEV, LEN, 2))(jax.random.split(arg_keys[4], N_SEQ)).reshape((N_SEQ, PROMPTS_DEV)).astype(jnp.int32)
    variate_ids = set_ends(jax.random.randint(arg_keys[5], (TOKENS,), 0, NVAR), jax.random.fold_in(arg_keys[5], 1), 0, NVAR - 1).astype(jnp.int32)
    variate_bias = draw_variate_bias(jax.random.fold_in(arg_keys[7], 71), 0)
    return {"trainer_rows": trainer_rows, "shard_order": shard_order, "residual_in": residual_in, "norm_gains": norm_gains, "prompt_lengths": prompt_lengths, "variate_ids": variate_ids, "variate_bias": variate_bias}


NEGATIVE = -1e+30
EPSILON = 1e-05

def rms_scaled(values, gain):
    mean_square = lax.optimization_barrier(jnp.mean(values * values, axis=-1, keepdims=True))
    return values * lax.rsqrt(mean_square + EPSILON) * gain

def rotate(values, offsets):
    half_width = values.shape[-1] // 2
    frequency = 10000.0 ** (-jnp.arange(half_width, dtype=jnp.float32) / half_width)
    angles = offsets.astype(jnp.float32)[:, None] * frequency[None, :]
    cosine = jnp.cos(angles)[:, None, :]
    sine_part = jnp.sin(angles)[:, None, :]
    front_half = values[..., :half_width]
    back_half = values[..., half_width:]
    return jnp.concatenate([front_half * cosine - back_half * sine_part, front_half * sine_part + back_half * cosine], axis=-1)

def prompt_layout(lengths, token_count):
    prompt_ends = jnp.cumsum(lengths).astype(jnp.int32)
    prompt_starts = (prompt_ends - lengths).astype(jnp.int32)
    positions = jnp.arange(token_count, dtype=jnp.int32)
    segment = lax.optimization_barrier(jnp.sum((positions[:, None] >= prompt_ends[None, :]).astype(jnp.int32), axis=1)).astype(jnp.int32)
    member = segment[:, None] == jnp.arange(lengths.shape[0], dtype=jnp.int32)[None, :]
    offsets = (positions - lax.optimization_barrier(jnp.sum(jnp.where(member, prompt_starts[None, :], 0), axis=1))).astype(jnp.int32)
    return (segment, offsets)

def group_sum(source, weight_t):
    group_width = source.shape[1] // N_TP
    terms = jnp.einsum('tgw,dgw->gtd', source.reshape(source.shape[0], N_TP, group_width).astype(jnp.float32), weight_t.reshape(weight_t.shape[0], N_TP, group_width).astype(jnp.float32))
    rounded = lax.optimization_barrier(terms.astype(jnp.bfloat16))
    return lax.optimization_barrier(jnp.sum(rounded.astype(jnp.float32), axis=0))

def reference(trainer_rows, shard_order, residual_in, norm_gains, prompt_lengths, variate_ids, variate_bias):
    blocks = trainer_rows.reshape(LAYERS, DEVICES, D // DEVICES, 4 * D + 3 * FF)
    placed = jnp.zeros_like(blocks).at[:, shard_order].set(blocks)
    weights = placed.reshape(LAYERS, D, 4 * D + 3 * FF).astype(jnp.bfloat16)

    def one_block(inputs):
        residual, lengths, variates = inputs
        segment, offsets = prompt_layout(lengths, TOK_DEV)
        same_prompt = segment[:, None] == segment[None, :]
        same_variate = variates[:, None] == variates[None, :]
        for layer_index in range(LAYERS):
            layer_bias = variate_bias[layer_index]
            pair_bias = jnp.where(same_variate[None], layer_bias[:, 1][:, None, None], layer_bias[:, 0][:, None, None])
            layer_weights = weights[layer_index]
            normed = rms_scaled(residual, norm_gains[layer_index, 0]).astype(jnp.bfloat16)
            projected = jnp.dot(normed, layer_weights[:, :3 * D], preferred_element_type=jnp.float32)
            queries = rotate(projected[:, :D].reshape(TOK_DEV, H, HD), offsets).astype(jnp.bfloat16)
            key_rows = rotate(projected[:, D:2 * D].reshape(TOK_DEV, H, HD), offsets).astype(jnp.bfloat16)
            values = projected[:, 2 * D:3 * D].reshape(TOK_DEV, H, HD).astype(jnp.bfloat16)
            scores = jnp.einsum('qhd,khd->hqk', queries.astype(jnp.float32), key_rows.astype(jnp.float32)) * HD ** (-0.5) + pair_bias
            scores = jnp.where(same_prompt[None], scores, NEGATIVE)
            row_peak = lax.optimization_barrier(jnp.max(scores, axis=2, keepdims=True))
            weights_exp = jnp.exp(scores - row_peak)
            attn_weights = (weights_exp / lax.optimization_barrier(jnp.sum(weights_exp, axis=2, keepdims=True))).astype(jnp.bfloat16)
            mixed_heads = jnp.einsum('hqk,khd->qhd', attn_weights.astype(jnp.float32), values.astype(jnp.float32)).astype(jnp.bfloat16).reshape(TOK_DEV, D)
            residual = residual + group_sum(mixed_heads, layer_weights[:, 3 * D:4 * D])
            normed_mlp = rms_scaled(residual, norm_gains[layer_index, 1]).astype(jnp.bfloat16)
            gate_up = jnp.dot(normed_mlp, layer_weights[:, 4 * D:4 * D + 2 * FF], preferred_element_type=jnp.float32)
            hidden = (jax.nn.silu(gate_up[:, :FF]) * gate_up[:, FF:]).astype(jnp.bfloat16)
            residual = residual + group_sum(hidden, layer_weights[:, 4 * D + 2 * FF:])
        return residual
    outputs = lax.map(one_block, (residual_in.reshape(N_SEQ, TOK_DEV, D), prompt_lengths, variate_ids.reshape(N_SEQ, TOK_DEV)))
    return outputs.reshape(TOK_DEV * N_SEQ, D)
```

```python
import functools

import jax
import jax.numpy as jnp
from jax import lax
from jax.experimental import pallas as pl
from jax.experimental.pallas import tpu as pltpu
from jax.sharding import PartitionSpec as P

NEGATIVE = -1e30
EPSILON = 1e-05


def rms_scaled(values, gain):
    mean_square = jnp.mean(values * values, axis=-1, keepdims=True)
    return values * lax.rsqrt(mean_square + EPSILON) * gain


def rotate(values, offsets):
    half_width = values.shape[-1] // 2
    frequency = 10000.0 ** (-jnp.arange(half_width, dtype=jnp.float32) / half_width)
    angles = offsets.astype(jnp.float32)[:, None] * frequency[None, :]
    cosine = jnp.cos(angles)[:, None, :]
    sine_part = jnp.sin(angles)[:, None, :]
    front_half = values[..., :half_width]
    back_half = values[..., half_width:]
    return jnp.concatenate(
        [front_half * cosine - back_half * sine_part, front_half * sine_part + back_half * cosine],
        axis=-1,
    )


def prompt_layout(lengths, token_count):
    order = jnp.arange(lengths.shape[0])
    prompt_ends = jnp.sum(
        jnp.where(order[:, None] >= order[None, :], lengths[None, :], 0), axis=1
    )
    prompt_starts = prompt_ends - lengths
    positions = jnp.arange(token_count, dtype=jnp.int32)
    segment = jnp.sum((positions[:, None] >= prompt_ends[None, :]).astype(jnp.int32), axis=1)
    member = segment[:, None] == jnp.arange(lengths.shape[0], dtype=jnp.int32)[None, :]
    offsets = positions - jnp.sum(jnp.where(member, prompt_starts[None, :], 0), axis=1)
    return (segment, offsets)


def project_rows(row_piece, weight):
    return jnp.dot(row_piece, weight, preferred_element_type=jnp.float32)


def gated_units(row_piece, weight):
    gate_up = jnp.dot(row_piece, weight, preferred_element_type=jnp.float32)
    half_width = weight.shape[1] // 2
    return (jax.nn.silu(gate_up[:, :half_width]) * gate_up[:, half_width:]).astype(jnp.bfloat16)


def project_out(source, weight):
    return lax.dot_general(
        source, weight, (((1,), (1,)), ((), ())), preferred_element_type=jnp.float32
    )


CHUNKS = 2
MESH = pl.DeviceIdType.MESH


def exchange_kernel(n, reduce, gather, *refs):
    refs = list(refs)
    part = refs.pop(0) if reduce else None
    residual = refs.pop(0)
    gain = refs.pop(0) if gather else None
    new_residual = refs.pop(0) if reduce else None
    gathered = refs.pop(0) if gather else None
    if reduce:
        slots, part_sent, part_got = refs[:3]
        refs = refs[3:]
    if gather:
        held, norm_sent, norm_got = refs
    rows = residual.shape[0]
    step = rows // CHUNKS
    me = lax.axis_index("tp")
    seq = lax.axis_index("seq")
    peers = [lax.rem(me + k, n) for k in range(1, n)]

    barrier = pltpu.get_barrier_semaphore()
    for peer in peers:
        pl.semaphore_signal(barrier, inc=1, device_id=(seq, peer), device_id_type=MESH)
    pl.semaphore_wait(barrier, n - 1)

    part_copies, norm_copies = [], []
    if reduce:
        for c in range(CHUNKS):
            for k in range(n - 1):
                start = pl.multiple_of(peers[k] * rows + c * step, step)
                copy = pltpu.make_async_remote_copy(
                    src_ref=part.at[pl.ds(start, step)],
                    dst_ref=slots.at[c, k],
                    send_sem=part_sent.at[c, k],
                    recv_sem=part_got.at[c, k],
                    device_id=(seq, peers[k]),
                    device_id_type=MESH,
                )
                copy.start()
                part_copies.append(copy)
    for c in range(CHUNKS):
        mine = pl.ds(pl.multiple_of(me * rows + c * step, step), step)
        values = residual[pl.ds(c * step, step)]
        if reduce:
            total = part[mine].astype(jnp.float32)
            for k in range(n - 1):
                part_copies[c * (n - 1) + k].wait_recv()
                total = total + slots[c, k].astype(jnp.float32)
            values = values + total
            new_residual[pl.ds(c * step, step)] = values
        if gather:
            held[mine] = rms_scaled(values, gain[...]).astype(jnp.bfloat16)
            for k in range(n - 1):
                copy = pltpu.make_async_remote_copy(
                    src_ref=held.at[mine],
                    dst_ref=held.at[mine],
                    send_sem=norm_sent.at[c, k],
                    recv_sem=norm_got.at[c, k],
                    device_id=(seq, peers[k]),
                    device_id_type=MESH,
                )
                copy.start()
                norm_copies.append(copy)
    for copy in norm_copies:
        copy.wait_recv()
    if gather:
        gathered[...] = held[...]
    for copy in part_copies + norm_copies:
        copy.wait_send()


def exchange(n, residual, part=None, gain=None):
    reduce, gather = part is not None, gain is not None
    rows, width = residual.shape
    args = [residual]
    outs, scratch = [], []
    copies = pltpu.SemaphoreType.DMA((CHUNKS, n - 1))
    if reduce:
        args = [part] + args
        outs.append(jax.ShapeDtypeStruct((rows, width), jnp.float32))
        scratch += [pltpu.VMEM((CHUNKS, n - 1, rows // CHUNKS, width), jnp.bfloat16), copies, copies]
    if gather:
        args.append(gain)
        outs.append(jax.ShapeDtypeStruct((n * rows, width), jnp.bfloat16))
        scratch += [pltpu.VMEM((n * rows, width), jnp.bfloat16), copies, copies]
    vmem = pl.BlockSpec(memory_space=pltpu.VMEM)
    sides = int(reduce) + int(gather)
    return pl.pallas_call(
        functools.partial(exchange_kernel, n, reduce, gather),
        out_shape=outs,
        in_specs=[vmem] * len(args),
        out_specs=[vmem] * len(outs),
        scratch_shapes=scratch,
        compiler_params=pltpu.CompilerParams(
            collective_id=int(reduce) + 2 * int(gather),
            has_side_effects=True,
            vmem_limit_bytes=24 * 1024 * 1024,
        ),
        cost_estimate=pl.CostEstimate(
            flops=10 * rows * width,
            bytes_accessed=sides * 64 * 1024 * 1024,
            transcendentals=0,
        ),
    )(*args)


def permuted(values, matrix):
    return jnp.dot(
        values, matrix, precision=lax.Precision.HIGHEST, preferred_element_type=jnp.float32
    )


def on_device(
    trainer_rows, shard_order, residual_in, norm_gains, prompt_lengths, variate_ids, variate_bias
):
    tp_count = lax.axis_size("tp")
    seq_count = lax.axis_size("seq")
    layer_count, block_rows, total_cols = trainer_rows.shape
    model_width = residual_in.shape[1]
    ff_width = (total_cols - 4 * model_width) // 3
    head_cols = model_width // tp_count
    unit_cols = ff_width // tp_count
    widths = [model_width] * 4 + [ff_width] * 3
    starts = [sum(widths[:i]) for i in range(len(widths))]

    def by_owner(layer, parts):
        pieces = []
        for i in parts:
            piece = trainer_rows[layer, :, starts[i] : starts[i] + widths[i]].astype(jnp.bfloat16)
            pieces.append(
                piece.reshape(block_rows, tp_count, widths[i] // tp_count).transpose(1, 0, 2)
            )
        return pieces

    def swap(pieces):
        swapped = lax.all_to_all(
            jnp.concatenate(pieces, axis=2), "tp", split_axis=0, concat_axis=1, tiled=True
        )
        return swapped[0]

    def over_seq(piece):
        return lax.all_gather(piece, "seq", axis=0, tiled=True)

    first = over_seq(swap(by_owner(0, range(4))))
    later = by_owner(0, range(4, 7))
    for layer in range(1, layer_count):
        later = later + by_owner(layer, range(7))
    later = swap(later)
    attention_weights, mlp_weights = [first], []
    at = 0
    for layer in range(layer_count):
        if layer > 0:
            attention_weights.append(over_seq(later[:, at : at + 4 * head_cols]))
            at = at + 4 * head_cols
        mlp_weights.append(over_seq(later[:, at : at + 3 * unit_cols]))
        at = at + 3 * unit_cols

    column = jnp.arange(model_width, dtype=jnp.int32)
    rows_in_block = model_width // shard_order.shape[0]
    row_of = (
        shard_order[:, None] * rows_in_block
        + jnp.arange(rows_in_block, dtype=jnp.int32)[None, :]
    ).reshape(model_width)
    to_trainer = (column[:, None] == row_of[None, :]).astype(jnp.float32)
    gains = permuted(norm_gains.reshape(2 * layer_count, model_width), to_trainer)
    token_count = variate_ids.shape[0]
    segment, offsets = prompt_layout(prompt_lengths[0], token_count)
    same_prompt = segment[:, None] == segment[None, :]
    same_variate = variate_ids[:, None] == variate_ids[None, :]
    head_count = variate_bias.shape[1]
    local_heads = head_count // tp_count
    head_size = head_cols // local_heads
    bias_table = lax.dynamic_slice_in_dim(
        variate_bias, lax.axis_index("tp") * local_heads, local_heads, 1
    )
    residual = permuted(residual_in, to_trainer)
    [gathered] = exchange(tp_count, residual, gain=gains[:1])
    for layer_index in range(layer_count):
        layer_bias = bias_table[layer_index]
        pair_bias = jnp.where(
            same_variate[None], layer_bias[:, 1][:, None, None], layer_bias[:, 0][:, None, None]
        )
        layer_weights = attention_weights[layer_index]
        qkv_weight = layer_weights[:, : 3 * head_cols]
        out_weight = layer_weights[:, 3 * head_cols :]
        layer_weights = mlp_weights[layer_index]
        gate_up_weight = layer_weights[:, : 2 * unit_cols]
        down_weight = layer_weights[:, 2 * unit_cols :]
        projected = project_rows(gathered, weight=qkv_weight)
        queries = rotate(
            projected[:, :head_cols].reshape(token_count, local_heads, head_size), offsets
        ).astype(jnp.bfloat16)
        key_rows = rotate(
            projected[:, head_cols : 2 * head_cols].reshape(token_count, local_heads, head_size),
            offsets,
        ).astype(jnp.bfloat16)
        values = (
            projected[:, 2 * head_cols : 3 * head_cols]
            .reshape(token_count, local_heads, head_size)
            .astype(jnp.bfloat16)
        )
        scores = (
            jnp.einsum("qhd,khd->hqk", queries, key_rows, preferred_element_type=jnp.float32)
            * head_size ** (-0.5)
            + pair_bias
        )
        scores = jnp.where(same_prompt[None], scores, NEGATIVE)
        row_peak = jnp.max(scores, axis=2, keepdims=True)
        weights_exp = jnp.exp(scores - row_peak)
        attn_weights = (weights_exp / jnp.sum(weights_exp, axis=2, keepdims=True)).astype(
            jnp.bfloat16
        )
        mixed_heads = (
            jnp.einsum("hqk,khd->qhd", attn_weights, values, preferred_element_type=jnp.float32)
            .astype(jnp.bfloat16)
            .reshape(token_count, head_cols)
        )
        head_part = project_out(source=mixed_heads, weight=out_weight).astype(jnp.bfloat16)
        residual, gathered = exchange(
            tp_count, residual, head_part, gains[2 * layer_index + 1 : 2 * layer_index + 2]
        )
        hidden = gated_units(gathered, weight=gate_up_weight)
        unit_part = project_out(source=hidden, weight=down_weight).astype(jnp.bfloat16)
        if layer_index + 1 < layer_count:
            residual, gathered = exchange(
                tp_count, residual, unit_part, gains[2 * layer_index + 2 : 2 * layer_index + 3]
            )
        else:
            [residual] = exchange(tp_count, residual, unit_part)
    return permuted(residual, to_trainer.T)


def solution(mesh):
    return jax.shard_map(
        on_device,
        mesh=mesh,
        in_specs=(
            P(None, ("seq", "tp"), None),
            P(),
            P(("seq", "tp"), None),
            P(),
            P("seq", None),
            P("seq"),
            P(),
        ),
        out_specs=P(("seq", "tp"), None),
        check_vma=False,
    )
```

```python
import functools

import jax
import jax.numpy as jnp
from jax import lax
from jax.experimental import pallas as pl
from jax.experimental.pallas import tpu as pltpu
from jax.sharding import PartitionSpec as P

NEGATIVE = -1e30
EPSILON = 1e-05


def rms_scaled(values, gain):
    mean_square = jnp.mean(values * values, axis=-1, keepdims=True)
    return values * lax.rsqrt(mean_square + EPSILON) * gain


def rotate(values, offsets):
    half_width = values.shape[-1] // 2
    frequency = 10000.0 ** (-jnp.arange(half_width, dtype=jnp.float32) / half_width)
    angles = offsets.astype(jnp.float32)[:, None] * frequency[None, :]
    cosine = jnp.cos(angles)[:, None, :]
    sine_part = jnp.sin(angles)[:, None, :]
    front_half = values[..., :half_width]
    back_half = values[..., half_width:]
    return jnp.concatenate(
        [front_half * cosine - back_half * sine_part, front_half * sine_part + back_half * cosine],
        axis=-1,
    )


def prompt_layout(lengths, token_count):
    order = jnp.arange(lengths.shape[0])
    prompt_ends = jnp.sum(
        jnp.where(order[:, None] >= order[None, :], lengths[None, :], 0), axis=1
    )
    prompt_starts = prompt_ends - lengths
    positions = jnp.arange(token_count, dtype=jnp.int32)
    segment = jnp.sum((positions[:, None] >= prompt_ends[None, :]).astype(jnp.int32), axis=1)
    member = segment[:, None] == jnp.arange(lengths.shape[0], dtype=jnp.int32)[None, :]
    offsets = positions - jnp.sum(jnp.where(member, prompt_starts[None, :], 0), axis=1)
    return (segment, offsets)


def project_rows(row_piece, weight):
    return jnp.dot(row_piece, weight, preferred_element_type=jnp.float32)


def gated_units(row_piece, weight):
    gate_up = jnp.dot(row_piece, weight, preferred_element_type=jnp.float32)
    half_width = weight.shape[1] // 2
    return (jax.nn.silu(gate_up[:, :half_width]) * gate_up[:, half_width:]).astype(jnp.bfloat16)


def project_out(source, weight):
    return lax.dot_general(
        source, weight, (((1,), (1,)), ((), ())), preferred_element_type=jnp.float32
    )


CHUNKS = 2
MESH = pl.DeviceIdType.MESH


def exchange_kernel(n, reduce, gather, *refs):
    refs = list(refs)
    part = refs.pop(0) if reduce else None
    residual = refs.pop(0)
    gain = refs.pop(0) if gather else None
    new_residual = refs.pop(0) if reduce else None
    gathered = refs.pop(0) if gather else None
    if reduce:
        slots, part_sent, part_got = refs[:3]
        refs = refs[3:]
    if gather:
        held, norm_sent, norm_got = refs
    rows = residual.shape[0]
    step = rows // CHUNKS
    me = lax.axis_index("tp")
    seq = lax.axis_index("seq")
    peers = [lax.rem(me + k, n) for k in range(1, n)]

    barrier = pltpu.get_barrier_semaphore()
    for peer in peers:
        pl.semaphore_signal(barrier, inc=1, device_id=(seq, peer), device_id_type=MESH)
    pl.semaphore_wait(barrier, n - 1)

    part_copies, norm_copies = [], []
    if reduce:
        for c in range(CHUNKS):
            for k in range(n - 1):
                start = pl.multiple_of(peers[k] * rows + c * step, step)
                copy = pltpu.make_async_remote_copy(
                    src_ref=part.at[pl.ds(start, step)],
                    dst_ref=slots.at[c, k],
                    send_sem=part_sent.at[c, k],
                    recv_sem=part_got.at[c, k],
                    device_id=(seq, peers[k]),
                    device_id_type=MESH,
                )
                copy.start()
                part_copies.append(copy)
    for c in range(CHUNKS):
        mine = pl.ds(pl.multiple_of(me * rows + c * step, step), step)
        values = residual[pl.ds(c * step, step)]
        if reduce:
            total = part[mine].astype(jnp.float32)
            for k in range(n - 1):
                part_copies[c * (n - 1) + k].wait_recv()
                total = total + slots[c, k].astype(jnp.float32)
            values = values + total
            new_residual[pl.ds(c * step, step)] = values
        if gather:
            held[mine] = rms_scaled(values, gain[...]).astype(jnp.bfloat16)
            for k in range(n - 1):
                copy = pltpu.make_async_remote_copy(
                    src_ref=held.at[mine],
                    dst_ref=held.at[mine],
                    send_sem=norm_sent.at[c, k],
                    recv_sem=norm_got.at[c, k],
                    device_id=(seq, peers[k]),
                    device_id_type=MESH,
                )
                copy.start()
                norm_copies.append(copy)
    for copy in norm_copies:
        copy.wait_recv()
    if gather:
        gathered[...] = held[...]
    for copy in part_copies + norm_copies:
        copy.wait_send()


def square_kernel(reduce, gather, *refs):
    refs = list(refs)
    part = refs.pop(0) if reduce else None
    residual = refs.pop(0)
    gain = refs.pop(0) if gather else None
    new_residual = refs.pop(0) if reduce else None
    gathered = refs.pop(0) if gather else None
    if reduce:
        slots, onward, part_sent, part_got = refs[:4]
        refs = refs[4:]
    if gather:
        held, norm_sent, norm_got = refs
    rows, width = residual.shape
    step = rows // CHUNKS
    half = width // 2
    front, back = pl.ds(0, half), pl.ds(half, half)
    me = lax.axis_index("tp")
    seq = lax.axis_index("seq")
    major, minor = lax.div(me, 2), lax.rem(me, 2)
    beside = major * 2 + (1 - minor)
    above = (1 - major) * 2 + minor
    across = (1 - major) * 2 + (1 - minor)

    barrier = pltpu.get_barrier_semaphore()
    for peer in (beside, above):
        pl.semaphore_signal(barrier, inc=1, device_id=(seq, peer), device_id_type=MESH)
    pl.semaphore_wait(barrier, 2)

    def of(owner, c):
        return pl.ds(pl.multiple_of(owner * rows + c * step, step), step)

    started = []

    def send(source, target, sent, got, peer):
        copy = pltpu.make_async_remote_copy(
            src_ref=source,
            dst_ref=target,
            send_sem=sent,
            recv_sem=got,
            device_id=(seq, peer),
            device_id_type=MESH,
        )
        copy.start()
        started.append(copy)
        return copy

    def send_part(kind, c, source, peer):
        return send(source, slots.at[kind, c], part_sent.at[kind, c], part_got.at[kind, c], peer)

    if reduce:
        relay, own, passed = [], [], []
        for c in range(CHUNKS):
            relay.append(
                (
                    send_part(0, c, part.at[of(across, c), front], beside),
                    send_part(1, c, part.at[of(across, c), back], above),
                )
            )
        for c in range(CHUNKS):
            own.append(
                (
                    send_part(2, c, part.at[of(beside, c), front], beside),
                    send_part(3, c, part.at[of(above, c), back], above),
                )
            )
        for c in range(CHUNKS):
            pair = []
            for side, columns, owner in ((0, front, above), (1, back, beside)):
                relay[c][side].wait_recv()
                onward[side, c] = (
                    part[of(owner, c), columns].astype(jnp.float32)
                    + slots[side, c].astype(jnp.float32)
                ).astype(jnp.bfloat16)
                pair.append(send_part(4 + side, c, onward.at[side, c], owner))
            passed.append(pair)
    whole = []
    for c in range(CHUNKS):
        here = pl.ds(c * step, step)
        if reduce:
            for side, columns in ((0, front), (1, back)):
                own[c][side].wait_recv()
                passed[c][side].wait_recv()
                new_residual[here, columns] = residual[here, columns] + (
                    part[of(me, c), columns].astype(jnp.float32)
                    + slots[2 + side, c].astype(jnp.float32)
                    + slots[4 + side, c].astype(jnp.float32)
                )
        if gather:
            values = new_residual[here] if reduce else residual[here]
            mine = held.at[of(me, c)]
            held[of(me, c)] = rms_scaled(values, gain[...]).astype(jnp.bfloat16)
            whole.append(
                (
                    send(mine, mine, norm_sent.at[0, c], norm_got.at[0, c], beside),
                    send(mine, mine, norm_sent.at[1, c], norm_got.at[1, c], above),
                )
            )
    if gather:
        halves = []
        for c in range(CHUNKS):
            for side, columns, source, peer in (
                (0, front, beside, above),
                (1, back, above, beside),
            ):
                whole[c][side].wait_recv()
                piece = held.at[of(source, c), columns]
                halves.append(
                    send(piece, piece, norm_sent.at[2 + side, c], norm_got.at[2 + side, c], peer)
                )
        for copy in halves:
            copy.wait_recv()
        gathered[...] = held[...]
    for copy in started:
        copy.wait_send()


def exchange(n, residual, part=None, gain=None):
    reduce, gather = part is not None, gain is not None
    rows, width = residual.shape
    args = [residual]
    outs, scratch = [], []
    square = n == 4
    part_copies = pltpu.SemaphoreType.DMA((6, CHUNKS) if square else (CHUNKS, n - 1))
    norm_copies = pltpu.SemaphoreType.DMA((4, CHUNKS) if square else (CHUNKS, n - 1))
    if reduce:
        args = [part] + args
        outs.append(jax.ShapeDtypeStruct((rows, width), jnp.float32))
        step = rows // CHUNKS
        if square:
            scratch.append(pltpu.VMEM((6, CHUNKS, step, width // 2), jnp.bfloat16))
            scratch.append(pltpu.VMEM((2, CHUNKS, step, width // 2), jnp.bfloat16))
        else:
            scratch.append(pltpu.VMEM((CHUNKS, n - 1, step, width), jnp.bfloat16))
        scratch += [part_copies, part_copies]
    if gather:
        args.append(gain)
        outs.append(jax.ShapeDtypeStruct((n * rows, width), jnp.bfloat16))
        scratch += [pltpu.VMEM((n * rows, width), jnp.bfloat16), norm_copies, norm_copies]
    vmem = pl.BlockSpec(memory_space=pltpu.VMEM)
    sides = int(reduce) + int(gather)
    return pl.pallas_call(
        functools.partial(square_kernel, reduce, gather)
        if square
        else functools.partial(exchange_kernel, n, reduce, gather),
        out_shape=outs,
        in_specs=[vmem] * len(args),
        out_specs=[vmem] * len(outs),
        scratch_shapes=scratch,
        compiler_params=pltpu.CompilerParams(
            collective_id=int(reduce) + 2 * int(gather),
            has_side_effects=True,
            vmem_limit_bytes=24 * 1024 * 1024,
        ),
        cost_estimate=pl.CostEstimate(
            flops=10 * rows * width,
            bytes_accessed=sides * 64 * 1024 * 1024,
            transcendentals=0,
        ),
    )(*args)


def permuted(values, matrix):
    return jnp.dot(
        values, matrix, precision=lax.Precision.HIGHEST, preferred_element_type=jnp.float32
    )


def on_device(
    trainer_rows, shard_order, residual_in, norm_gains, prompt_lengths, variate_ids, variate_bias
):
    tp_count = lax.axis_size("tp")
    seq_count = lax.axis_size("seq")
    layer_count, block_rows, total_cols = trainer_rows.shape
    model_width = residual_in.shape[1]
    ff_width = (total_cols - 4 * model_width) // 3
    head_cols = model_width // tp_count
    unit_cols = ff_width // tp_count
    widths = [model_width] * 4 + [ff_width] * 3
    starts = [sum(widths[:i]) for i in range(len(widths))]

    def by_owner(layer, parts):
        pieces = []
        for i in parts:
            piece = trainer_rows[layer, :, starts[i] : starts[i] + widths[i]].astype(jnp.bfloat16)
            pieces.append(
                piece.reshape(block_rows, tp_count, widths[i] // tp_count).transpose(1, 0, 2)
            )
        return pieces

    def swap(pieces):
        swapped = lax.all_to_all(
            jnp.concatenate(pieces, axis=2), "tp", split_axis=0, concat_axis=1, tiled=True
        )
        return swapped[0]

    def over_seq(piece):
        return lax.all_gather(piece, "seq", axis=0, tiled=True)

    first = over_seq(swap(by_owner(0, range(4))))
    later = by_owner(0, range(4, 7))
    for layer in range(1, layer_count):
        later = later + by_owner(layer, range(7))
    later = swap(later)
    attention_weights, mlp_weights = [first], []
    at = 0
    for layer in range(layer_count):
        if layer > 0:
            attention_weights.append(over_seq(later[:, at : at + 4 * head_cols]))
            at = at + 4 * head_cols
        mlp_weights.append(over_seq(later[:, at : at + 3 * unit_cols]))
        at = at + 3 * unit_cols

    column = jnp.arange(model_width, dtype=jnp.int32)
    rows_in_block = model_width // shard_order.shape[0]
    row_of = (
        shard_order[:, None] * rows_in_block
        + jnp.arange(rows_in_block, dtype=jnp.int32)[None, :]
    ).reshape(model_width)
    to_trainer = (column[:, None] == row_of[None, :]).astype(jnp.float32)
    gains = permuted(norm_gains.reshape(2 * layer_count, model_width), to_trainer)
    token_count = variate_ids.shape[0]
    segment, offsets = prompt_layout(prompt_lengths[0], token_count)
    same_prompt = segment[:, None] == segment[None, :]
    same_variate = variate_ids[:, None] == variate_ids[None, :]
    head_count = variate_bias.shape[1]
    local_heads = head_count // tp_count
    head_size = head_cols // local_heads
    bias_table = lax.dynamic_slice_in_dim(
        variate_bias, lax.axis_index("tp") * local_heads, local_heads, 1
    )
    residual = permuted(residual_in, to_trainer)
    [gathered] = exchange(tp_count, residual, gain=gains[:1])
    for layer_index in range(layer_count):
        layer_bias = bias_table[layer_index]
        pair_bias = jnp.where(
            same_variate[None], layer_bias[:, 1][:, None, None], layer_bias[:, 0][:, None, None]
        )
        layer_weights = attention_weights[layer_index]
        qkv_weight = layer_weights[:, : 3 * head_cols]
        out_weight = layer_weights[:, 3 * head_cols :]
        layer_weights = mlp_weights[layer_index]
        gate_up_weight = layer_weights[:, : 2 * unit_cols]
        down_weight = layer_weights[:, 2 * unit_cols :]
        projected = project_rows(gathered, weight=qkv_weight)
        queries = rotate(
            projected[:, :head_cols].reshape(token_count, local_heads, head_size), offsets
        ).astype(jnp.bfloat16)
        key_rows = rotate(
            projected[:, head_cols : 2 * head_cols].reshape(token_count, local_heads, head_size),
            offsets,
        ).astype(jnp.bfloat16)
        values = (
            projected[:, 2 * head_cols : 3 * head_cols]
            .reshape(token_count, local_heads, head_size)
            .astype(jnp.bfloat16)
        )
        scores = (
            jnp.einsum("qhd,khd->hqk", queries, key_rows, preferred_element_type=jnp.float32)
            * head_size ** (-0.5)
            + pair_bias
        )
        scores = jnp.where(same_prompt[None], scores, NEGATIVE)
        row_peak = jnp.max(scores, axis=2, keepdims=True)
        weights_exp = jnp.exp(scores - row_peak)
        attn_weights = (weights_exp / jnp.sum(weights_exp, axis=2, keepdims=True)).astype(
            jnp.bfloat16
        )
        mixed_heads = (
            jnp.einsum("hqk,khd->qhd", attn_weights, values, preferred_element_type=jnp.float32)
            .astype(jnp.bfloat16)
            .reshape(token_count, head_cols)
        )
        head_part = project_out(source=mixed_heads, weight=out_weight).astype(jnp.bfloat16)
        residual, gathered = exchange(
            tp_count, residual, head_part, gains[2 * layer_index + 1 : 2 * layer_index + 2]
        )
        hidden = gated_units(gathered, weight=gate_up_weight)
        unit_part = project_out(source=hidden, weight=down_weight).astype(jnp.bfloat16)
        if layer_index + 1 < layer_count:
            residual, gathered = exchange(
                tp_count, residual, unit_part, gains[2 * layer_index + 2 : 2 * layer_index + 3]
            )
        else:
            [residual] = exchange(tp_count, residual, unit_part)
    return permuted(residual, to_trainer.T)


def solution(mesh):
    return jax.shard_map(
        on_device,
        mesh=mesh,
        in_specs=(
            P(None, ("seq", "tp"), None),
            P(),
            P(("seq", "tp"), None),
            P(),
            P("seq", None),
            P("seq"),
            P(),
        ),
        out_specs=P(("seq", "tp"), None),
        check_vma=False,
    )
```
